32 devices in a mesh: chan: 2 (over x), src: 16 (over z, y, core).
Axes of the slice: x: 2, y: 2, z: 4, core: 2. Of those that a mesh axis runs over, the one named last changes fastest.
Arguments:
- intensity: float32 [65536], P(('chan', 'src')), parts along dimension 0, may hold values from 0.25 to 4
- directions: float32 [4, 3, 32768], P(None, None, 'src'), may hold values from -1 to 1
- positions: float32 [6, 350], P('chan'), parts along dimension 0, may hold values from -20 to 20
- beam: bfloat16 [350, 512], P(None, 'src'), may hold values from 0.19921875 to 1
- need: int32 [4, 128], P(None, 'src'), may hold values from 0 to 31
- knot_index: int32 [4, 4, 32768], P(None, None, 'src'), may hold values from 0 to 127
- knot_weight: float32 [4, 4, 32768], P(None, None, 'src'), may hold values from 0 to 1
- pairs: int32 [2, 7680], P(None, 'src'), may hold values from 0 to 349, as said below
Outputs:
- vis: float32 [8, 2, 7680], P('chan', None, 'src'), parts along dimension 0
The draws below stay inside these ranges and needn't reach their ends.
There are 2 independent parts, one for each index of `chan`. The reference program is written for one: setup_inputs(seed, part) draws one part's arguments, and reference() takes and returns one part's arrays. A program takes and returns all parts, laid end to end along the dimension named above; an argument that names none is the same for every part. Nothing has to cross between parts.
Inputs may be any that keep to these rules, and one draw needn't show every extreme that they name: `pairs`: each listed pair names two antennas, the first below the second.
All inputs are finite; a program needn't handle non-finite values.
Results may differ from the reference program's by a relative error of at most 0.004.
Values may be sent and summed in bfloat16 or wider, within the bound.
A program may use at most 256 MiB of HBM per device.

```python
import math
import jax
import jax.numpy as jnp
from jax import lax

RECEIVER_TOTAL = 350
S_DEV = 2048
SOURCES = 32768
TIME_STEPS = 4
BP_DEV = 32
BEAM_PIXELS = 512
PATCH_PIXELS = 16
NEED = 8
KNOTS = 4
PAIRING_TOTAL = 7680
N_SRC = 16


def draw_pairs(key, part):
    key = jax.random.fold_in(key, 11)
    leading_receiver_seed, second_antenna_key = jax.random.split(key)
    first_antenna = jax.random.randint(leading_receiver_seed, (PAIRING_TOTAL,), 0, RECEIVER_TOTAL - 1)
    patch_offset = jax.random.randint(second_antenna_key, (PAIRING_TOTAL,), 1, RECEIVER_TOTAL - first_antenna)
    second_antenna = first_antenna + patch_offset
    baseline_place = jnp.arange(PAIRING_TOTAL)
    first_antenna = jnp.where(baseline_place == 0, 0, first_antenna)
    second_antenna = jnp.where(baseline_place == 0, RECEIVER_TOTAL - 1, second_antenna)
    return jnp.stack([first_antenna, second_antenna]).astype(jnp.int32)


def set_ends(values, key, low, largest):
    longest = values.shape.index(max(values.shape))
    spots = []
    for shift in (0, 1):
        where = [jax.random.randint(jax.random.fold_in(key, axis), (), 0, length) for axis, length in enumerate(values.shape)]
        where[longest] = (where[longest] + shift) % values.shape[longest]
        spots.append(tuple(where))
    return values.at[spots[0]].set(low).at[spots[1]].set(largest)


def block_levels(key, dims, shards, smallest, high):
    level = 1.0
    for position, blocks in shards:
        draws = jax.random.uniform(jax.random.fold_in(jax.random.fold_in(key, 6), position), (blocks,), jnp.float32, smallest / len(shards), high / len(shards))
        level = level * jnp.repeat(jnp.exp(draws), dims[position] // blocks).reshape((-1,) + (1,) * (len(dims) - 1 - position))
    return level


def setup_inputs(seed: int = 0, part: int = 0) -> dict:
    seeds = jax.random.split(jax.random.key(seed), 9)
    part_keys = jax.random.split(jax.random.fold_in(seeds[8], part), 9)
    intensity = jnp.clip(jnp.exp(math.log(4.0) - 2.7725887 * jax.random.uniform(part_keys[0], (SOURCES,), jnp.float32) ** block_levels(part_keys[0], (SOURCES,), ((0, 16),), -0.2, 0.2)), 0.25, 4.0)
    directions = jnp.clip(jax.random.uniform(seeds[1], (TIME_STEPS, 3, SOURCES), jnp.float32, -1.0, 1.0) * block_levels(seeds[1], (TIME_STEPS, 3, SOURCES), ((2, 16),), -0.4, 0.0), -1.0, 1.0)
    positions = jnp.clip(jax.random.uniform(part_keys[2], (3, RECEIVER_TOTAL), jnp.float32, -20.0, 20.0), -20.0, 20.0)
    beam = jnp.clip(0.19921875 + 0.80078125 * jax.random.uniform(seeds[3], (RECEIVER_TOTAL, BEAM_PIXELS), jnp.float32) ** block_levels(seeds[3], (RECEIVER_TOTAL, BEAM_PIXELS), ((1, 16),), -0.2, 0.2), 0.19921875, 1.0).astype(jnp.bfloat16)
    need = set_ends(jax.random.randint(seeds[4], (TIME_STEPS, NEED * N_SRC), 0, BP_DEV * N_SRC // PATCH_PIXELS), jax.random.fold_in(seeds[4], 1), 0, (BP_DEV * N_SRC // PATCH_PIXELS) - 1).astype(jnp.int32)
    knot_index = set_ends(jax.random.randint(seeds[5], (TIME_STEPS, KNOTS, SOURCES), 0, NEED * PATCH_PIXELS), jax.random.fold_in(seeds[5], 1), 0, (NEED * PATCH_PIXELS) - 1).astype(jnp.int32)
    knot_weight = jnp.clip(1.0 * jax.random.uniform(seeds[6], (TIME_STEPS, KNOTS, SOURCES), jnp.float32) ** block_levels(seeds[6], (TIME_STEPS, KNOTS, SOURCES), ((2, 16),), -0.2, 0.2), 0.0, 1.0)
    pairs = draw_pairs(jax.random.fold_in(seeds[8], 71), part)
    return {"intensity": intensity, "directions": directions, "positions": positions, "beam": beam, "need": need, "knot_index": knot_index, "knot_weight": knot_weight, "pairs": pairs}


def tile_gram(intensity, directions, positions, beam, need, knot_index, knot_weight):
    scale = float(SOURCES) ** (-0.25)
    amplitude = jnp.sqrt(intensity) * scale
    result = []
    for time_step in range(TIME_STEPS):
        slot = knot_index[time_step]
        pixel = need[time_step][slot // PATCH_PIXELS] * PATCH_PIXELS + slot % PATCH_PIXELS
        values = jnp.take(beam, pixel, axis=1)
        response = lax.optimization_barrier(jnp.sum(values.astype(jnp.float32) * knot_weight[time_step][None], axis=1))
        phase = 2.0 * math.pi * jnp.dot(positions.T, directions[time_step], precision=lax.Precision.HIGHEST, preferred_element_type=jnp.float32)
        interpolation_factor = response * amplitude[None]
        stacked = jnp.concatenate([interpolation_factor * jnp.cos(phase), -interpolation_factor * jnp.sin(phase)], axis=0).astype(jnp.bfloat16)
        inner_product_table = lax.dot_general(stacked, stacked, (((1,), (1,)), ((), ())), preferred_element_type=jnp.float32)
        antenna_list = positions.shape[1]
        real_values = inner_product_table[:antenna_list, :antenna_list] + inner_product_table[antenna_list:, antenna_list:]
        imaginary_values = inner_product_table[antenna_list:, :antenna_list] - inner_product_table[:antenna_list, antenna_list:]
        result.append(jnp.stack([real_values, imaginary_values]))
    return jnp.stack(result)

def reference(intensity, directions, positions, beam, need, knot_index, knot_weight, pairs):
    tiles = SOURCES // S_DEV
    antenna_list = positions.shape[1]
    brightness_broadcast = intensity.reshape(tiles, S_DEV)
    dir_b = jnp.moveaxis(directions.reshape(TIME_STEPS, 3, tiles, S_DEV), 2, 0)
    need_b = jnp.moveaxis(need.reshape(TIME_STEPS, tiles, NEED), 1, 0)
    index_b = jnp.moveaxis(knot_index.reshape(TIME_STEPS, KNOTS, tiles, S_DEV), 2, 0)
    weight_b = jnp.moveaxis(knot_weight.reshape(TIME_STEPS, KNOTS, tiles, S_DEV), 2, 0)

    def add_tile(total, pieces):
        inten, dirs, needs, index, interpolation_factors = pieces
        return (total + tile_gram(inten, dirs, positions, beam, needs, index, interpolation_factors), None)
    patch_start = jnp.zeros((TIME_STEPS, 2, antenna_list, antenna_list), jnp.float32)
    total, _ = lax.scan(add_tile, patch_start, (brightness_broadcast, dir_b, need_b, index_b, weight_b))
    return total[:, :, pairs[0], pairs[1]]
```

```python
import jax
import jax.numpy as jnp
from jax import lax
from jax.experimental import pallas as pl
from jax.experimental.pallas import tpu as pltpu
from jax.sharding import PartitionSpec as P

TIME_STEPS = 4
PATCH_PIXELS = 16
NEED = 8
KNOTS = 4
SLOTS = NEED * PATCH_PIXELS
CHUNK = 512
BF = jnp.bfloat16
F32 = jnp.float32
MAGIC = 12582912.0

SIN = (4.4428679, -7.30744342, 3.59478805, -0.78437398)
COS = (-1.41420408, 6.97764205, -5.71523832, 1.72834847)


def nt(a, b):
    return lax.dot_general(a, b, (((1,), (1,)), ((), ())), preferred_element_type=F32)


def pieces(x):
    hi = x.astype(BF).astype(F32)
    mid = (x - hi).astype(BF).astype(F32)
    return hi, mid, (x - hi) - mid


def gram_kernel(scale, ants, rows, wide, need_ref, intensity_ref, directions_ref, positions_ref, beam_ref,
                index_ref, weight_ref, out_ref, pos, beam_sel, amp, s0, s1, gram):
    count = intensity_ref.shape[1]
    chunks = count // CHUNK
    amp[...] = jnp.sqrt(intensity_ref[...]) * scale
    s0[...] = jnp.zeros_like(s0)
    s1[...] = jnp.zeros_like(s1)
    gram[...] = jnp.zeros_like(gram)
    p0, p1, p2 = pieces(positions_ref[...])
    pos[...] = jnp.concatenate([p0, p0, p1, p1, p0, p2], axis=0).T.astype(BF)
    slots = (s0, s1)
    iota = lax.broadcasted_iota(jnp.int32, (SLOTS, CHUNK), 0)

    def fill(t, c, slot):
        lanes = pl.ds(c * CHUNK, CHUNK)
        d0, d1, d2 = pieces(directions_ref[t, :, lanes])
        d = jnp.concatenate([d0, d1, d0, d1, d2, d0], axis=0).astype(BF)
        u = jnp.dot(pos[:rows], d, preferred_element_type=F32)
        spread = jnp.zeros((SLOTS, CHUNK), F32)
        a = amp[:, lanes]
        for k in range(KNOTS):
            w = weight_ref[t, pl.ds(k, 1), lanes] * a
            spread = spread + jnp.where(iota == index_ref[t, pl.ds(k, 1), lanes], w, 0.0)
        hi = spread.astype(BF)
        lo = (spread - hi.astype(F32)).astype(BF)
        b = beam_sel[:rows]
        amount = jnp.dot(
            jnp.concatenate([b, b], axis=1), jnp.concatenate([hi, lo], axis=0), preferred_element_type=F32
        )
        r = u - ((u + MAGIC) - MAGIC)
        z = r * r
        s = (((SIN[3] * z + SIN[2]) * z + SIN[1]) * z + SIN[0]) * r
        n = ((COS[3] * z + COS[2]) * z + COS[1]) * z + COS[0]
        q = amount * s
        slot[:rows] = (amount - q * s).astype(BF)
        slot[wide : wide + rows] = (q * n).astype(BF)

    def add(slot):
        for lo in range(0, 2 * wide, 256):
            hi = min(lo + 256, 2 * wide)
            cols = slot[lo:hi]
            if lo < rows:
                gram[lo:rows, lo:hi] += nt(slot[lo:rows], cols)
            top = max(lo, wide)
            gram[top : wide + rows, lo:hi] += nt(slot[top : wide + rows], cols)

    def finish(t):
        w = gram[wide:, :wide]
        real = gram[:wide, :wide] + gram[wide:, wide:]
        r = lax.broadcasted_iota(jnp.int32, (wide, wide), 0)
        c = lax.broadcasted_iota(jnp.int32, (wide, wide), 1)
        out_ref[t] = jnp.where(r > c, real, w - w.T)
        gram[...] = jnp.zeros_like(gram)

    def body(t, carry):
        picked = [
            beam_ref[pl.ds(pl.multiple_of(need_ref[t, j] * PATCH_PIXELS, PATCH_PIXELS), PATCH_PIXELS), :]
            for j in range(NEED)
        ]
        beam_sel[...] = jnp.concatenate(picked, axis=0).astype(F32).T.astype(BF)
        for c in range(chunks):
            fill(t, c, slots[c % 2])
            add(slots[(c + 1) % 2])
            if c == 0:
                @pl.when(t > 0)
                def _():
                    finish(t - 1)
        return carry

    lax.fori_loop(0, TIME_STEPS, body, 0)
    add(slots[(chunks - 1) % 2])
    finish(TIME_STEPS - 1)


def pick_kernel(pairs_ref, total_ref, out_ref):
    wide = total_ref.shape[1]
    count = pairs_ref.shape[1]
    iota = lax.broadcasted_iota(jnp.int32, (wide, count), 0)
    first = iota == pairs_ref[0:1, :]
    second = iota == pairs_ref[1:2, :]
    one0 = jnp.where(first, 1.0, 0.0).astype(BF)
    one1 = jnp.where(second, 1.0, 0.0).astype(BF)
    for t in range(TIME_STEPS):
        v = total_ref[t]
        hi = v.astype(BF)
        lo = (v - hi.astype(F32)).astype(BF)
        both = jnp.concatenate([hi, lo], axis=1)
        for part, (one, mask) in enumerate(((one0, second), (one1, first))):
            x = jnp.dot(both, jnp.concatenate([one, one], axis=0), preferred_element_type=F32)
            out_ref[t, part : part + 1, :] = jnp.sum(jnp.where(mask, x, 0.0), axis=0, keepdims=True)


def local(intensity, directions, positions, beam, need, knot_index, knot_weight, pairs):
    ants = positions.shape[1]
    rows = -(-ants // 16) * 16
    wide = -(-ants // 128) * 128
    count = intensity.shape[0]
    scale = float(count * lax.axis_size("src")) ** (-0.25)
    mine = jnp.pad(beam.T, ((0, 0), (0, wide - ants)))
    whole = lax.all_gather(mine, "src", axis=0, tiled=True)
    spaced = jnp.pad(positions, ((0, 5), (0, wide - ants)))
    aimed = jnp.pad(directions, ((0, 0), (0, 5), (0, 0)))
    vmem = pl.BlockSpec(memory_space=pltpu.VMEM)
    part = pl.pallas_call(
        lambda *refs: gram_kernel(scale, ants, rows, wide, *refs),
        out_shape=jax.ShapeDtypeStruct((TIME_STEPS, wide, wide), F32),
        in_specs=[pl.BlockSpec(memory_space=pltpu.SMEM)] + [vmem] * 6,
        out_specs=vmem,
        scratch_shapes=[
            pltpu.VMEM((wide, 48), BF),
            pltpu.VMEM((wide, SLOTS), BF),
            pltpu.VMEM((1, count), F32),
            pltpu.VMEM((2 * wide, CHUNK), BF),
            pltpu.VMEM((2 * wide, CHUNK), BF),
            pltpu.VMEM((2 * wide, 2 * wide), F32),
        ],
        compiler_params=pltpu.CompilerParams(vmem_limit_bytes=56 * 1024 * 1024),
    )(need, intensity.reshape(1, count), aimed, spaced, whole, knot_index, knot_weight)
    total = lax.psum(part, "src")
    return pl.pallas_call(
        pick_kernel,
        out_shape=jax.ShapeDtypeStruct((TIME_STEPS, 2, pairs.shape[1]), F32),
        in_specs=[vmem, vmem],
        out_specs=vmem,
        compiler_params=pltpu.CompilerParams(vmem_limit_bytes=56 * 1024 * 1024),
    )(pairs, total)


def solution(mesh):
    placed = (
        P(("chan", "src")),
        P(None, None, "src"),
        P("chan", None),
        P(None, "src"),
        P(None, "src"),
        P(None, None, "src"),
        P(None, None, "src"),
        P(None, "src"),
    )
    return jax.shard_map(
        local, mesh=mesh, in_specs=placed, out_specs=P("chan", None, "src"), check_vma=False
    )
```

```python
import jax
import jax.numpy as jnp
from jax import lax
from jax.experimental import pallas as pl
from jax.experimental.pallas import tpu as pltpu
from jax.sharding import PartitionSpec as P

TIME_STEPS = 4
PATCH_PIXELS = 16
NEED = 8
KNOTS = 4
SLOTS = NEED * PATCH_PIXELS
CHUNK = 512
BF = jnp.bfloat16
F32 = jnp.float32
MAGIC = 12582912.0

SIN = (4.4428679, -7.30744342, 3.59478805, -0.78437398)
COS = (-1.41420408, 6.97764205, -5.71523832, 1.72834847)


def nt(a, b):
    return lax.dot_general(a, b, (((1,), (1,)), ((), ())), preferred_element_type=F32)


def pieces(x):
    hi = x.astype(BF).astype(F32)
    mid = (x - hi).astype(BF).astype(F32)
    return hi, mid, (x - hi) - mid


def gram_kernel(scale, ants, rows, wide, need_ref, intensity_ref, directions_ref, positions_ref, beam_ref,
                index_ref, weight_ref, out_ref, pos, beam_sel, amp, s0, s1, gram):
    count = intensity_ref.shape[1]
    chunks = count // CHUNK
    amp[...] = jnp.sqrt(intensity_ref[...]) * scale
    s0[...] = jnp.zeros_like(s0)
    s1[...] = jnp.zeros_like(s1)
    gram[...] = jnp.zeros_like(gram)
    p0, p1, p2 = pieces(positions_ref[...])
    pos[...] = jnp.concatenate([p0, p0, p1, p1, p0, p2], axis=0).T.astype(BF)
    slots = (s0, s1)
    iota = lax.broadcasted_iota(jnp.int32, (SLOTS, CHUNK), 0)

    def fill(t, c, slot):
        lanes = pl.ds(c * CHUNK, CHUNK)
        d0, d1, d2 = pieces(directions_ref[t, :, lanes])
        d = jnp.concatenate([d0, d1, d0, d1, d2, d0], axis=0).astype(BF)
        u = jnp.dot(pos[:rows], d, preferred_element_type=F32)
        spread = jnp.zeros((SLOTS, CHUNK), F32)
        a = amp[:, lanes]
        for k in range(KNOTS):
            w = weight_ref[t, pl.ds(k, 1), lanes] * a
            spread = spread + jnp.where(iota == index_ref[t, pl.ds(k, 1), lanes], w, 0.0)
        hi = spread.astype(BF)
        lo = (spread - hi.astype(F32)).astype(BF)
        b = beam_sel[:rows]
        amount = jnp.dot(
            jnp.concatenate([b, b], axis=1), jnp.concatenate([hi, lo], axis=0), preferred_element_type=F32
        )
        r = u - ((u + MAGIC) - MAGIC)
        z = r * r
        s = (((SIN[3] * z + SIN[2]) * z + SIN[1]) * z + SIN[0]) * r
        n = ((COS[3] * z + COS[2]) * z + COS[1]) * z + COS[0]
        q = amount * s
        slot[:rows] = (amount - q * s).astype(BF)
        slot[wide : wide + rows] = (q * n).astype(BF)

    def add(slot):
        for lo in range(0, 2 * wide, 256):
            hi = min(lo + 256, 2 * wide)
            cols = slot[lo:hi]
            if lo < rows:
                gram[lo:rows, lo:hi] += nt(slot[lo:rows], cols)
            top = max(lo, wide)
            gram[top : wide + rows, lo:hi] += nt(slot[top : wide + rows], cols)

    def finish(t):
        w = gram[wide:, :wide]
        real = gram[:wide, :wide] + gram[wide:, wide:]
        r = lax.broadcasted_iota(jnp.int32, (wide, wide), 0)
        c = lax.broadcasted_iota(jnp.int32, (wide, wide), 1)
        out_ref[t] = jnp.where(r > c, real, w - w.T)
        gram[...] = jnp.zeros_like(gram)

    def body(t, carry):
        picked = [
            beam_ref[pl.ds(pl.multiple_of(need_ref[t, j] * PATCH_PIXELS, PATCH_PIXELS), PATCH_PIXELS), :]
            for j in range(NEED)
        ]
        beam_sel[...] = jnp.concatenate(picked, axis=0).astype(F32).T.astype(BF)
        for c in range(chunks):
            fill(t, c, slots[c % 2])
            add(slots[(c + 1) % 2])
            if c == 0:
                @pl.when(t > 0)
                def _():
                    finish(t - 1)
        return carry

    lax.fori_loop(0, TIME_STEPS, body, 0)
    add(slots[(chunks - 1) % 2])
    finish(TIME_STEPS - 1)


def partners(size):
    me = lax.axis_index("src")
    flips = [1 << bit for bit in range(size.bit_length() - 1)]
    return me, flips


def flip(me, value):
    return me + value - 2 * value * (lax.div(me, value) % 2)


def greet(others):
    barrier = pltpu.get_barrier_semaphore()
    for other in others:
        pl.semaphore_signal(barrier, inc=1, device_id={"src": other}, device_id_type=pl.DeviceIdType.MESH)
    pl.semaphore_wait(barrier, len(others))


def push(src, dst, send, recv, other):
    copy = pltpu.make_async_remote_copy(
        src_ref=src, dst_ref=dst, send_sem=send, recv_sem=recv,
        device_id={"src": other}, device_id_type=pl.DeviceIdType.MESH,
    )
    copy.start()
    return copy


def reverse(index, bits):
    out = 0
    for bit in range(bits):
        out = out + (index // (1 << bit)) % 2 * (1 << (bits - 1 - bit))
    return out


def spread_kernel(size, beam_ref, pairs_ref, whole_ref, quad_ref, sems, quad_sems):
    me, flips = partners(size)
    bits = len(flips)
    quad = [flip(me, 1), flip(me, 2), flip(flip(me, 1), 2)]
    slot = reverse(me, bits)
    whole_ref[slot] = beam_ref[...]
    quad_ref[me % 4] = pairs_ref[...]
    greet([flip(me, value) for value in flips[2:]] + quad)
    copies = []
    for j, other in enumerate(quad):
        copies.append(push(pairs_ref, quad_ref.at[me % 4], quad_sems.at[0, j], quad_sems.at[1, j], other))
    for stage in range(bits):
        held = 1 << stage
        blocks = whole_ref.at[pl.ds(slot // held * held, held)]
        push(blocks, blocks, sems.at[0, stage], sems.at[1, stage], flip(me, flips[bits - 1 - stage])).wait()
    for copy in copies:
        copy.wait()


def total_kernel(size, part_ref, quad_ref, out_ref, ones, got0, send1, got1, acc, sends, gots, res, got, sem0, sem1, sems,
                 quad_sems):
    me, flips = partners(size)
    wide = part_ref.shape[1]
    half, quarter = wide // 2, wide // 4
    count = quad_ref.shape[2]
    core, side = me % 2, me // 2 % 2
    quad = [flip(me, 1), flip(me, 2), flip(flip(me, 1), 2)]
    greet([flip(me, value) for value in flips[2:]] + quad)
    first = []
    for t in range(TIME_STEPS):
        away = part_ref.at[t, pl.ds(pl.multiple_of((1 - core) * half, 64), half)]
        first.append(push(away, got0.at[t], sem0.at[0, t], sem0.at[1, t], quad[0]))
    iota = lax.broadcasted_iota(jnp.int32, (wide, count), 0)
    for m in range(4):
        for k in range(2):
            ones[m, k] = jnp.where(iota == quad_ref[m, k : k + 1, :], 1.0, 0.0).astype(BF)
    mine = pl.multiple_of(core * half + side * quarter, 32)
    theirs = pl.multiple_of(core * half + (1 - side) * quarter, 32)
    in_mine = pl.multiple_of(side * quarter, 32)
    in_theirs = pl.multiple_of((1 - side) * quarter, 32)
    second = []
    for t in range(TIME_STEPS):
        first[t].wait()
        send1[t] = (part_ref[t, pl.ds(theirs, quarter)] + got0[t, pl.ds(in_theirs, quarter)]).astype(BF)
        second.append(push(send1.at[t], got1.at[t], sem1.at[0, t], sem1.at[1, t], quad[1]))
    for t in range(TIME_STEPS):
        acc[t] = part_ref[t, pl.ds(mine, quarter)] + got0[t, pl.ds(in_mine, quarter)]
    waiting = second
    for stage, value in enumerate(flips[2:]):
        later = []
        for t in range(TIME_STEPS):
            waiting[t].wait()
            arrived = got1[t] if stage == 0 else gots[stage - 1, t]
            v = acc[t] + arrived.astype(F32)
            acc[t] = v
            sends[stage, t] = v.astype(BF)
            later.append(push(sends.at[stage, t], gots.at[stage, t], sems.at[0, stage, t], sems.at[1, stage, t], flip(me, value)))
        waiting = later
    for t in range(TIME_STEPS):
        waiting[t].wait()
    rows = (acc[...] + gots[len(flips) - 3].astype(F32)).astype(BF).reshape(TIME_STEPS * quarter, wide)
    local_iota = lax.broadcasted_iota(jnp.int32, (quarter, count), 0) + mine
    member = me % 4
    for m in range(4):
        for k in range(2):
            x = jnp.dot(rows, ones[m, 1 - k], preferred_element_type=F32)
            mask = local_iota == quad_ref[m, k : k + 1, :]
            for t in range(TIME_STEPS):
                y = jnp.where(mask, x[t * quarter : (t + 1) * quarter], 0.0)
                res[m, 2 * t + 1 - k : 2 * t + 2 - k, :] = jnp.sum(y, axis=0, keepdims=True)
    last = []
    for j, other in enumerate(quad):
        last.append(push(res.at[other % 4], got.at[j], quad_sems.at[0, j], quad_sems.at[1, j], other))
    for copy in last:
        copy.wait()
    out_ref[...] = res[member] + got[0] + got[1] + got[2]


def local(intensity, directions, positions, beam, need, knot_index, knot_weight, pairs):
    ants = positions.shape[1]
    rows = -(-ants // 16) * 16
    wide = -(-ants // 128) * 128
    count = intensity.shape[0]
    scale = float(count * lax.axis_size("src")) ** (-0.25)
    mine = jnp.pad(beam.T, ((0, 0), (0, wide - ants)))
    size = lax.axis_size("src")
    bits = size.bit_length() - 1
    vmem = pl.BlockSpec(memory_space=pltpu.VMEM)
    whole, quad = pl.pallas_call(
        lambda *refs: spread_kernel(size, *refs),
        out_shape=(
            jax.ShapeDtypeStruct((size,) + mine.shape, BF),
            jax.ShapeDtypeStruct((4,) + pairs.shape, jnp.int32),
        ),
        in_specs=[vmem, vmem],
        out_specs=(vmem, vmem),
        scratch_shapes=[pltpu.SemaphoreType.DMA((2, bits)), pltpu.SemaphoreType.DMA((2, 3))],
        compiler_params=pltpu.CompilerParams(collective_id=0, has_side_effects=True),
    )(mine, pairs)
    parts = mine.shape[0] // PATCH_PIXELS
    need = reverse(need // parts, bits) * parts + need % parts
    whole = whole.reshape(-1, wide)
    spaced = jnp.pad(positions, ((0, 5), (0, wide - ants)))
    aimed = jnp.pad(directions, ((0, 0), (0, 5), (0, 0)))
    part = pl.pallas_call(
        lambda *refs: gram_kernel(scale, ants, rows, wide, *refs),
        out_shape=jax.ShapeDtypeStruct((TIME_STEPS, wide, wide), F32),
        in_specs=[pl.BlockSpec(memory_space=pltpu.SMEM)] + [vmem] * 6,
        out_specs=vmem,
        scratch_shapes=[
            pltpu.VMEM((wide, 48), BF),
            pltpu.VMEM((wide, SLOTS), BF),
            pltpu.VMEM((1, count), F32),
            pltpu.VMEM((2 * wide, CHUNK), BF),
            pltpu.VMEM((2 * wide, CHUNK), BF),
            pltpu.VMEM((2 * wide, 2 * wide), F32),
        ],
        compiler_params=pltpu.CompilerParams(vmem_limit_bytes=56 * 1024 * 1024),
    )(need, intensity.reshape(1, count), aimed, spaced, whole, knot_index, knot_weight)
    half, quarter, pair_count = wide // 2, wide // 4, pairs.shape[1]
    dma = pltpu.SemaphoreType.DMA
    out = pl.pallas_call(
        lambda *refs: total_kernel(size, *refs),
        out_shape=jax.ShapeDtypeStruct((2 * TIME_STEPS, pair_count), F32),
        in_specs=[vmem, vmem],
        out_specs=vmem,
        scratch_shapes=[
            pltpu.VMEM((4, 2, wide, pair_count), BF),
            pltpu.VMEM((TIME_STEPS, half, wide), F32),
            pltpu.VMEM((TIME_STEPS, quarter, wide), BF),
            pltpu.VMEM((TIME_STEPS, quarter, wide), BF),
            pltpu.VMEM((TIME_STEPS, quarter, wide), F32),
            pltpu.VMEM((bits - 2, TIME_STEPS, quarter, wide), BF),
            pltpu.VMEM((bits - 2, TIME_STEPS, quarter, wide), BF),
            pltpu.VMEM((4, 2 * TIME_STEPS, pair_count), F32),
            pltpu.VMEM((3, 2 * TIME_STEPS, pair_count), F32),
            dma((2, TIME_STEPS)),
            dma((2, TIME_STEPS)),
            dma((2, bits - 2, TIME_STEPS)),
            dma((2, 3)),
        ],
        compiler_params=pltpu.CompilerParams(
            collective_id=1, has_side_effects=True, vmem_limit_bytes=48 * 1024 * 1024
        ),
    )(part, quad)
    return out.reshape(TIME_STEPS, 2, pair_count)


def solution(mesh):
    placed = (
        P(("chan", "src")),
        P(None, None, "src"),
        P("chan", None),
        P(None, "src"),
        P(None, "src"),
        P(None, None, "src"),
        P(None, None, "src"),
        P(None, "src"),
    )
    return jax.shard_map(
        local, mesh=mesh, in_specs=placed, out_specs=P("chan", None, "src"), check_vma=False
    )
```

```python
import jax
import jax.numpy as jnp
from jax import lax
from jax.experimental import pallas as pl
from jax.experimental.pallas import tpu as pltpu
from jax.sharding import PartitionSpec as P

TIME_STEPS = 4
PATCH_PIXELS = 16
NEED = 8
KNOTS = 4
SLOTS = NEED * PATCH_PIXELS
CHUNK = 512
BF = jnp.bfloat16
F32 = jnp.float32
MAGIC = 12582912.0

SIN = (4.4428679, -7.30744342, 3.59478805, -0.78437398)
COS = (-1.41420408, 6.97764205, -5.71523832, 1.72834847)


def nt(a, b):
    return lax.dot_general(a, b, (((1,), (1,)), ((), ())), preferred_element_type=F32)


def pieces(x):
    hi = x.astype(BF).astype(F32)
    mid = (x - hi).astype(BF).astype(F32)
    return hi, mid, (x - hi) - mid


def partners(size):
    me = lax.axis_index("src")
    flips = [1 << bit for bit in range(size.bit_length() - 1)]
    return me, flips


def flip(me, value):
    return me + value - 2 * value * (lax.div(me, value) % 2)


def greet(others):
    barrier = pltpu.get_barrier_semaphore()
    for other in others:
        pl.semaphore_signal(barrier, inc=1, device_id={"src": other}, device_id_type=pl.DeviceIdType.MESH)
    pl.semaphore_wait(barrier, len(others))


def push(src, dst, send, recv, other):
    copy = pltpu.make_async_remote_copy(
        src_ref=src, dst_ref=dst, send_sem=send, recv_sem=recv,
        device_id={"src": other}, device_id_type=pl.DeviceIdType.MESH,
    )
    copy.start()
    return copy


def reverse(index, bits):
    out = 0
    for bit in range(bits):
        out = out + (index // (1 << bit)) % 2 * (1 << (bits - 1 - bit))
    return out


def kernel(size, scale, need_ref, intensity_ref, directions_ref, positions_ref, beam_ref, index_ref, weight_ref,
           pairs_ref, out_ref, whole, quads, pos, padded, block, dirs, beam_sel, amp, s0, s1, gram, kept_s, kept_n, part,
           ones, got0, send1, got1, acc, sends, gots, res, got, gsem, qsem, sem0, sem1, sems, rsem):
    me, flips = partners(size)
    bits = len(flips)
    count = intensity_ref.shape[1]
    chunks = count // CHUNK
    ants = positions_ref.shape[1]
    depth = beam_ref.shape[1]
    parts = depth // PATCH_PIXELS
    rows, wide = -(-ants // 16) * 16, whole.shape[2]
    half, quarter = wide // 2, wide // 4
    pair_count = pairs_ref.shape[1]
    core, side = me % 2, me // 2 % 2
    quad = [flip(me, 1), flip(me, 2), flip(flip(me, 1), 2)]

    slot_me = reverse(me, bits)
    block[...] = jnp.zeros_like(block)
    block[:ants, :depth] = beam_ref[...].astype(F32)
    whole[slot_me] = block[...].T[:depth].astype(BF)
    quads[me % 4] = pairs_ref[...]
    greet([flip(me, value) for value in flips[2:]] + quad)

    def gather_copy(stage):
        held = 1 << stage
        blocks = whole.at[pl.ds(slot_me // held * held, held)]
        return pltpu.make_async_remote_copy(
            src_ref=blocks, dst_ref=blocks, send_sem=gsem.at[0, stage], recv_sem=gsem.at[1, stage],
            device_id={"src": flip(me, flips[bits - 1 - stage])}, device_id_type=pl.DeviceIdType.MESH,
        )

    gather_copy(0).start()
    listed = [
        push(pairs_ref, quads.at[me % 4], qsem.at[0, j], qsem.at[1, j], other) for j, other in enumerate(quad)
    ]

    amp[...] = jnp.sqrt(intensity_ref[...]) * scale
    s0[...] = jnp.zeros_like(s0)
    s1[...] = jnp.zeros_like(s1)
    gram[...] = jnp.zeros_like(gram)
    dirs[...] = jnp.zeros_like(dirs)
    padded[...] = jnp.zeros_like(padded)
    padded[0:3, :ants] = positions_ref[...]
    p0, p1, p2 = pieces(padded[...])
    pos[...] = jnp.concatenate([p0, p0, p1, p1, p0, p2], axis=0).T.astype(BF)
    slots = (s0, s1)
    iota = lax.broadcasted_iota(jnp.int32, (SLOTS, CHUNK), 0)

    def fringe(t, c):
        lanes = pl.ds(c * CHUNK, CHUNK)
        d0, d1, d2 = pieces(directions_ref[t, :, lanes])
        for j, d in enumerate((d0, d1, d0, d1, d2, d0)):
            dirs[c % 2, 8 * j : 8 * j + 3] = d
        u = jnp.dot(pos[:rows], dirs[c % 2].astype(BF), preferred_element_type=F32)
        r = u - ((u + MAGIC) - MAGIC)
        z = r * r
        s = (((SIN[3] * z + SIN[2]) * z + SIN[1]) * z + SIN[0]) * r
        n = ((COS[3] * z + COS[2]) * z + COS[1]) * z + COS[0]
        return s, n

    def fill(t, c, slot, kept):
        lanes = pl.ds(c * CHUNK, CHUNK)
        spread = jnp.zeros((SLOTS, CHUNK), F32)
        a = amp[:, lanes]
        for k in range(KNOTS):
            w = weight_ref[t, pl.ds(k, 1), lanes] * a
            spread = spread + jnp.where(iota == index_ref[t, pl.ds(k, 1), lanes], w, 0.0)
        hi = spread.astype(BF)
        lo = (spread - hi.astype(F32)).astype(BF)
        b = beam_sel[:rows]
        amount = jnp.dot(
            jnp.concatenate([b, b], axis=1), jnp.concatenate([hi, lo], axis=0), preferred_element_type=F32
        )
        if kept:
            s, n = kept_s[:, lanes], kept_n[:, lanes]
        else:
            s, n = fringe(t, c)
        q = amount * s
        slot[:rows] = (amount - q * s).astype(BF)
        slot[wide : wide + rows] = (q * n).astype(BF)

    def add(slot):
        for lo in range(0, 2 * wide, 256):
            hi = min(lo + 256, 2 * wide)
            cols = slot[lo:hi]
            if lo < rows:
                gram[lo:rows, lo:hi] += nt(slot[lo:rows], cols)
            top = max(lo, wide)
            gram[top : wide + rows, lo:hi] += nt(slot[top : wide + rows], cols)

    def finish(t):
        w = gram[wide:, :wide]
        real = gram[:wide, :wide] + gram[wide:, wide:]
        r = lax.broadcasted_iota(jnp.int32, (wide, wide), 0)
        c = lax.broadcasted_iota(jnp.int32, (wide, wide), 1)
        part[t] = jnp.where(r > c, real, w - w.T)
        gram[...] = jnp.zeros_like(gram)

    mine = pl.multiple_of(core * half + side * quarter, 32)
    theirs = pl.multiple_of(core * half + (1 - side) * quarter, 32)
    in_mine = pl.multiple_of(side * quarter, 32)
    in_theirs = pl.multiple_of((1 - side) * quarter, 32)

    def remote(src, dst, send, recv, other):
        return pltpu.make_async_remote_copy(
            src_ref=src, dst_ref=dst, send_sem=send, recv_sem=recv,
            device_id={"src": other}, device_id_type=pl.DeviceIdType.MESH,
        )

    def core_copy(t):
        away = part.at[t, pl.ds(pl.multiple_of((1 - core) * half, 64), half)]
        return remote(away, got0.at[t], sem0.at[0, t], sem0.at[1, t], quad[0])

    def side_copy(t):
        return remote(send1.at[t], got1.at[t], sem1.at[0, t], sem1.at[1, t], quad[1])

    def far_copy(t, e):
        return remote(
            sends.at[e, t], gots.at[e, t], sems.at[0, e, t], sems.at[1, e, t], flip(me, flips[2 + e])
        )

    def to_side(t):
        core_copy(t).wait()
        send1[t] = (part[t, pl.ds(theirs, quarter)] + got0[t, pl.ds(in_theirs, quarter)]).astype(BF)
        side_copy(t).start()
        acc[t] = part[t, pl.ds(mine, quarter)] + got0[t, pl.ds(in_mine, quarter)]

    def to_far(t, e):
        if e == 0:
            side_copy(t).wait()
            v = acc[t] + got1[t].astype(F32)
        else:
            far_copy(t, e - 1).wait()
            v = acc[t] + gots[e - 1, t].astype(F32)
        acc[t] = v
        sends[e, t] = v.astype(BF)
        far_copy(t, e).start()

    for stage in range(max(bits, chunks)):
        if stage < chunks:
            lanes = pl.ds(stage * CHUNK, CHUNK)
            kept_s[:, lanes], kept_n[:, lanes] = fringe(0, stage)
        if stage < bits:
            gather_copy(stage).wait()
            if stage + 1 < bits:
                gather_copy(stage + 1).start()
    for copy in listed:
        copy.wait()

    pair_iota = lax.broadcasted_iota(jnp.int32, (wide, pair_count), 0)

    pixel = lax.broadcasted_iota(jnp.int32, (PATCH_PIXELS, size * depth), 1)
    row = lax.broadcasted_iota(jnp.int32, (PATCH_PIXELS, size * depth), 0)

    def choose(t):
        picked = []
        for j in range(NEED):
            patch = need_ref[t, j]
            at = reverse(patch // parts, bits) * depth + patch % parts * PATCH_PIXELS
            picked.append(jnp.where(pixel - row == at, 1.0, 0.0))
        hot = jnp.concatenate(picked, axis=0).astype(BF)
        got_rows = jnp.dot(hot, whole[...].reshape(size * depth, wide), preferred_element_type=F32)
        beam_sel[...] = got_rows.T.astype(BF)
        for k in range(2):
            ones[t, k] = jnp.where(pair_iota == quads[t, k : k + 1, :], 1.0, 0.0).astype(BF)

    choose(0)
    for c in range(chunks):
        fill(0, c, slots[c % 2], True)
        if c > 0:
            add(slots[(c + 1) % 2])

    def body(t, carry):
        choose(t)
        for c in range(chunks):
            fill(t, c, slots[c % 2], False)
            add(slots[(c + 1) % 2])
            if c == 0:
                finish(t - 1)
                core_copy(t - 1).start()

                @pl.when(t > 1)
                def _():
                    to_far(t - 2, 0)
            if c == 2:
                to_side(t - 1)

                @pl.when(t > 1)
                def _():
                    to_far(t - 2, 1)
        return carry

    lax.fori_loop(1, TIME_STEPS, body, 0)
    add(slots[(chunks - 1) % 2])
    finish(TIME_STEPS - 1)
    core_copy(TIME_STEPS - 1).start()
    far = bits - 2
    to_far(TIME_STEPS - 2, 0)
    to_side(TIME_STEPS - 1)
    to_far(TIME_STEPS - 2, 1)
    to_far(TIME_STEPS - 1, 0)
    to_far(TIME_STEPS - 1, 1)
    for e in range(2, far):
        for t in range(TIME_STEPS):
            to_far(t, e)
    for t in range(TIME_STEPS):
        far_copy(t, far - 1).wait()
    total = (acc[...] + gots[far - 1].astype(F32)).astype(BF).reshape(TIME_STEPS * quarter, wide)
    local_iota = lax.broadcasted_iota(jnp.int32, (quarter, pair_count), 0) + mine
    for m in range(4):
        for k in range(2):
            x = jnp.dot(total, ones[m, 1 - k], preferred_element_type=F32)
            mask = local_iota == quads[m, k : k + 1, :]
            for t in range(TIME_STEPS):
                y = jnp.where(mask, x[t * quarter : (t + 1) * quarter], 0.0)
                res[m, 2 * t + 1 - k : 2 * t + 2 - k, :] = jnp.sum(y, axis=0, keepdims=True)
    last = []
    for j, other in enumerate(quad):
        last.append(push(res.at[other % 4], got.at[j], rsem.at[0, j], rsem.at[1, j], other))
    for copy in last:
        copy.wait()
    values = res[me % 4] + got[0] + got[1] + got[2]
    for i in range(2 * TIME_STEPS):
        out_ref[i // 2, i % 2 : i % 2 + 1, :] = values[i : i + 1]


def local(intensity, directions, positions, beam, need, knot_index, knot_weight, pairs):
    ants = positions.shape[1]
    rows = -(-ants // 16) * 16
    wide = -(-ants // 128) * 128
    count = intensity.shape[0]
    size = lax.axis_size("src")
    scale = float(count * size) ** (-0.25)
    bits = size.bit_length() - 1
    half, quarter, pair_count = wide // 2, wide // 4, pairs.shape[1]
    vmem = pl.BlockSpec(memory_space=pltpu.VMEM)
    dma = pltpu.SemaphoreType.DMA
    return pl.pallas_call(
        lambda *refs: kernel(size, scale, *refs),
        out_shape=jax.ShapeDtypeStruct((TIME_STEPS, 2, pair_count), F32),
        in_specs=[pl.BlockSpec(memory_space=pltpu.SMEM)] + [vmem] * 7,
        out_specs=vmem,
        scratch_shapes=[
            pltpu.VMEM((size, beam.shape[1], wide), BF),
            pltpu.VMEM((4, 2, pair_count), jnp.int32),
            pltpu.VMEM((wide, 48), BF),
            pltpu.VMEM((8, wide), F32),
            pltpu.VMEM((wide, 128), F32),
            pltpu.VMEM((2, 48, CHUNK), F32),
            pltpu.VMEM((wide, SLOTS), BF),
            pltpu.VMEM((1, count), F32),
            pltpu.VMEM((2 * wide, CHUNK), BF),
            pltpu.VMEM((2 * wide, CHUNK), BF),
            pltpu.VMEM((2 * wide, 2 * wide), F32),
            pltpu.VMEM((rows, count), F32),
            pltpu.VMEM((rows, count), F32),
            pltpu.VMEM((TIME_STEPS, wide, wide), F32),
            pltpu.VMEM((4, 2, wide, pair_count), BF),
            pltpu.VMEM((TIME_STEPS, half, wide), F32),
            pltpu.VMEM((TIME_STEPS, quarter, wide), BF),
            pltpu.VMEM((TIME_STEPS, quarter, wide), BF),
            pltpu.VMEM((TIME_STEPS, quarter, wide), F32),
            pltpu.VMEM((bits - 2, TIME_STEPS, quarter, wide), BF),
            pltpu.VMEM((bits - 2, TIME_STEPS, quarter, wide), BF),
            pltpu.VMEM((4, 2 * TIME_STEPS, pair_count), F32),
            pltpu.VMEM((3, 2 * TIME_STEPS, pair_count), F32),
            dma((2, bits)),
            dma((2, 3)),
            dma((2, TIME_STEPS)),
            dma((2, TIME_STEPS)),
            dma((2, bits - 2, TIME_STEPS)),
            dma((2, 3)),
        ],
        compiler_params=pltpu.CompilerParams(
            collective_id=0, has_side_effects=True, vmem_limit_bytes=56 * 1024 * 1024
        ),
    )(need, intensity.reshape(1, count), directions, positions, beam, knot_index, knot_weight, pairs)


def solution(mesh):
    placed = (
        P(("chan", "src")),
        P(None, None, "src"),
        P("chan", None),
        P(None, "src"),
        P(None, "src"),
        P(None, None, "src"),
        P(None, None, "src"),
        P(None, "src"),
    )
    return jax.shard_map(
        local, mesh=mesh, in_specs=placed, out_specs=P("chan", None, "src"), check_vma=False
    )
```

```python
import jax
import jax.numpy as jnp
from jax import lax
from jax.experimental import pallas as pl
from jax.experimental.pallas import tpu as pltpu
from jax.sharding import PartitionSpec as P

TIME_STEPS = 4
PATCH_PIXELS = 16
NEED = 8
KNOTS = 4
SLOTS = NEED * PATCH_PIXELS
CHUNK = 512
BF = jnp.bfloat16
F32 = jnp.float32
MAGIC = 12582912.0

SIN = (4.4428679, -7.30744342, 3.59478805, -0.78437398)
COS = (-1.41420408, 6.97764205, -5.71523832, 1.72834847)


def nt(a, b):
    return lax.dot_general(a, b, (((1,), (1,)), ((), ())), preferred_element_type=F32)


def pieces(x):
    hi = x.astype(BF).astype(F32)
    mid = (x - hi).astype(BF).astype(F32)
    return hi, mid, (x - hi) - mid


def partners(size):
    me = lax.axis_index("src")
    flips = [1 << bit for bit in range(size.bit_length() - 1)]
    return me, flips


def flip(me, value):
    return me + value - 2 * value * (lax.div(me, value) % 2)


def greet(others):
    barrier = pltpu.get_barrier_semaphore()
    for other in others:
        pl.semaphore_signal(barrier, inc=1, device_id={"src": other}, device_id_type=pl.DeviceIdType.MESH)
    pl.semaphore_wait(barrier, len(others))


def push(src, dst, send, recv, other):
    copy = pltpu.make_async_remote_copy(
        src_ref=src, dst_ref=dst, send_sem=send, recv_sem=recv,
        device_id={"src": other}, device_id_type=pl.DeviceIdType.MESH,
    )
    copy.start()
    return copy


def reverse(index, bits):
    out = 0
    for bit in range(bits):
        out = out + (index // (1 << bit)) % 2 * (1 << (bits - 1 - bit))
    return out


def kernel(size, scale, need_ref, intensity_ref, directions_ref, positions_ref, beam_ref, index_ref, weight_ref,
           pairs_ref, out_ref, whole, quads, pos, padded, block, dirs, beam_sel, amp, s0, s1, gram, kept_s, kept_n, part,
           ones, got0, send1, got1, acc, sends, gots, res, got, gsem, qsem, sem0, sem1, sems, rsem):
    me, flips = partners(size)
    bits = len(flips)
    count = intensity_ref.shape[1]
    chunks = count // CHUNK
    ants = positions_ref.shape[1]
    depth = beam_ref.shape[1]
    parts = depth // PATCH_PIXELS
    rows, wide = -(-ants // 16) * 16, whole.shape[2]
    half, quarter = wide // 2, wide // 4
    pair_count = pairs_ref.shape[1]
    core, side = me % 2, me // 2 % 2
    quad = [flip(me, 1), flip(me, 2), flip(flip(me, 1), 2)]

    slot_me = reverse(me, bits)
    block[...] = jnp.zeros_like(block)
    block[:ants, :depth] = beam_ref[...].astype(F32)
    whole[slot_me] = block[...].T[:depth].astype(BF)
    quads[me % 4] = pairs_ref[...]
    greet([flip(me, value) for value in flips[2:]] + quad)

    def gather_copy(stage):
        held = 1 << stage
        blocks = whole.at[pl.ds(slot_me // held * held, held)]
        return pltpu.make_async_remote_copy(
            src_ref=blocks, dst_ref=blocks, send_sem=gsem.at[0, stage], recv_sem=gsem.at[1, stage],
            device_id={"src": flip(me, flips[bits - 1 - stage])}, device_id_type=pl.DeviceIdType.MESH,
        )

    gather_copy(0).start()
    listed = [
        push(pairs_ref, quads.at[me % 4], qsem.at[0, j], qsem.at[1, j], other) for j, other in enumerate(quad)
    ]

    amp[...] = jnp.sqrt(intensity_ref[...]) * scale
    s0[...] = jnp.zeros_like(s0)
    s1[...] = jnp.zeros_like(s1)
    gram[...] = jnp.zeros_like(gram)
    dirs[...] = jnp.zeros_like(dirs)
    padded[...] = jnp.zeros_like(padded)
    padded[0:3, :ants] = positions_ref[...]
    p0, p1, p2 = pieces(padded[...])
    pos[...] = jnp.concatenate([p0, p0, p1, p1, p0, p2], axis=0).T.astype(BF)
    slots = (s0, s1)
    iota = lax.broadcasted_iota(jnp.int32, (SLOTS, CHUNK), 0)

    def fringe(t, c, which):
        lanes = pl.ds(pl.multiple_of(c * CHUNK, CHUNK), CHUNK)
        d0, d1, d2 = pieces(directions_ref[t, :, lanes])
        for j, d in enumerate((d0, d1, d0, d1, d2, d0)):
            dirs[which, 8 * j : 8 * j + 3] = d
        u = jnp.dot(pos[:rows], dirs[which].astype(BF), preferred_element_type=F32)
        r = u - ((u + MAGIC) - MAGIC)
        z = r * r
        s = (((SIN[3] * z + SIN[2]) * z + SIN[1]) * z + SIN[0]) * r
        n = ((COS[3] * z + COS[2]) * z + COS[1]) * z + COS[0]
        kept_s[t, :, lanes] = s
        kept_n[t, :, lanes] = n

    def fill(t, c, slot):
        lanes = pl.ds(c * CHUNK, CHUNK)
        spread = jnp.zeros((SLOTS, CHUNK), F32)
        a = amp[:, lanes]
        for k in range(KNOTS):
            w = weight_ref[t, pl.ds(k, 1), lanes] * a
            spread = spread + jnp.where(iota == index_ref[t, pl.ds(k, 1), lanes], w, 0.0)
        hi = spread.astype(BF)
        lo = (spread - hi.astype(F32)).astype(BF)
        b = beam_sel[:rows]
        amount = jnp.dot(
            jnp.concatenate([b, b], axis=1), jnp.concatenate([hi, lo], axis=0), preferred_element_type=F32
        )
        s, n = kept_s[t, :, lanes], kept_n[t, :, lanes]
        q = amount * s
        slot[:rows] = (amount - q * s).astype(BF)
        slot[wide : wide + rows] = (q * n).astype(BF)

    def add(slot):
        for lo in range(0, 2 * wide, 256):
            hi = min(lo + 256, 2 * wide)
            cols = slot[lo:hi]
            if lo < rows:
                gram[lo:rows, lo:hi] += nt(slot[lo:rows], cols)
            top = max(lo, wide)
            gram[top : wide + rows, lo:hi] += nt(slot[top : wide + rows], cols)

    def finish(t):
        w = gram[wide:, :wide]
        real = gram[:wide, :wide] + gram[wide:, wide:]
        r = lax.broadcasted_iota(jnp.int32, (wide, wide), 0)
        c = lax.broadcasted_iota(jnp.int32, (wide, wide), 1)
        part[t] = jnp.where(r > c, real, w - w.T)
        gram[...] = jnp.zeros_like(gram)

    mine = pl.multiple_of(core * half + side * quarter, 32)
    theirs = pl.multiple_of(core * half + (1 - side) * quarter, 32)
    in_mine = pl.multiple_of(side * quarter, 32)
    in_theirs = pl.multiple_of((1 - side) * quarter, 32)

    def remote(src, dst, send, recv, other):
        return pltpu.make_async_remote_copy(
            src_ref=src, dst_ref=dst, send_sem=send, recv_sem=recv,
            device_id={"src": other}, device_id_type=pl.DeviceIdType.MESH,
        )

    def core_copy(t):
        away = part.at[t, pl.ds(pl.multiple_of((1 - core) * half, 64), half)]
        return remote(away, got0.at[t], sem0.at[0, t], sem0.at[1, t], quad[0])

    def side_copy(t):
        return remote(send1.at[t], got1.at[t], sem1.at[0, t], sem1.at[1, t], quad[1])

    def far_copy(t, e):
        return remote(
            sends.at[e, t], gots.at[e, t], sems.at[0, e, t], sems.at[1, e, t], flip(me, flips[2 + e])
        )

    def to_side(t):
        core_copy(t).wait()
        send1[t] = (part[t, pl.ds(theirs, quarter)] + got0[t, pl.ds(in_theirs, quarter)]).astype(BF)
        side_copy(t).start()
        acc[t] = part[t, pl.ds(mine, quarter)] + got0[t, pl.ds(in_mine, quarter)]

    def to_far(t, e):
        if e == 0:
            side_copy(t).wait()
            v = acc[t] + got1[t].astype(F32)
        else:
            far_copy(t, e - 1).wait()
            v = acc[t] + gots[e - 1, t].astype(F32)
        acc[t] = v
        sends[e, t] = v.astype(BF)
        far_copy(t, e).start()

    for stage in range(max(bits, TIME_STEPS)):
        if stage < TIME_STEPS:

            def some(c, carry, t=stage):
                fringe(t, 2 * c, 0)
                fringe(t, 2 * c + 1, 1)
                return carry

            lax.fori_loop(0, chunks // 2, some, 0)
        if stage < bits:
            gather_copy(stage).wait()
            if stage + 1 < bits:
                gather_copy(stage + 1).start()
    for copy in listed:
        copy.wait()

    pair_iota = lax.broadcasted_iota(jnp.int32, (wide, pair_count), 0)

    pixel = lax.broadcasted_iota(jnp.int32, (PATCH_PIXELS, size * depth), 1)
    row = lax.broadcasted_iota(jnp.int32, (PATCH_PIXELS, size * depth), 0)

    def choose(t):
        picked = []
        for j in range(NEED):
            patch = need_ref[t, j]
            at = reverse(patch // parts, bits) * depth + patch % parts * PATCH_PIXELS
            picked.append(jnp.where(pixel - row == at, 1.0, 0.0))
        hot = jnp.concatenate(picked, axis=0).astype(BF)
        got_rows = jnp.dot(hot, whole[...].reshape(size * depth, wide), preferred_element_type=F32)
        beam_sel[...] = got_rows.T.astype(BF)
        for k in range(2):
            ones[t, k] = jnp.where(pair_iota == quads[t, k : k + 1, :], 1.0, 0.0).astype(BF)

    choose(0)
    for c in range(chunks):
        fill(0, c, slots[c % 2])
        if c > 0:
            add(slots[(c + 1) % 2])

    def body(t, carry):
        choose(t)
        for c in range(chunks):
            fill(t, c, slots[c % 2])
            add(slots[(c + 1) % 2])
            if c == 0:
                finish(t - 1)
                core_copy(t - 1).start()

                @pl.when(t > 1)
                def _():
                    to_far(t - 2, 0)
            if c == 2:
                to_side(t - 1)

                @pl.when(t > 1)
                def _():
                    to_far(t - 2, 1)
        return carry

    lax.fori_loop(1, TIME_STEPS, body, 0)
    add(slots[(chunks - 1) % 2])
    finish(TIME_STEPS - 1)
    core_copy(TIME_STEPS - 1).start()
    far = bits - 2
    to_far(TIME_STEPS - 2, 0)
    to_side(TIME_STEPS - 1)
    to_far(TIME_STEPS - 2, 1)
    to_far(TIME_STEPS - 1, 0)
    to_far(TIME_STEPS - 1, 1)
    for e in range(2, far):
        for t in range(TIME_STEPS):
            to_far(t, e)
    for t in range(TIME_STEPS):
        far_copy(t, far - 1).wait()
    total = (acc[...] + gots[far - 1].astype(F32)).astype(BF).reshape(TIME_STEPS * quarter, wide)
    local_iota = lax.broadcasted_iota(jnp.int32, (quarter, pair_count), 0) + mine
    for m in range(4):
        for k in range(2):
            x = jnp.dot(total, ones[m, 1 - k], preferred_element_type=F32)
            mask = local_iota == quads[m, k : k + 1, :]
            for t in range(TIME_STEPS):
                y = jnp.where(mask, x[t * quarter : (t + 1) * quarter], 0.0)
                res[m, 2 * t + 1 - k : 2 * t + 2 - k, :] = jnp.sum(y, axis=0, keepdims=True)
    last = []
    for j, other in enumerate(quad):
        last.append(push(res.at[other % 4], got.at[j], rsem.at[0, j], rsem.at[1, j], other))
    for copy in last:
        copy.wait()
    values = res[me % 4] + got[0] + got[1] + got[2]
    for i in range(2 * TIME_STEPS):
        out_ref[i // 2, i % 2 : i % 2 + 1, :] = values[i : i + 1]


def local(intensity, directions, positions, beam, need, knot_index, knot_weight, pairs):
    ants = positions.shape[1]
    rows = -(-ants // 16) * 16
    wide = -(-ants // 128) * 128
    count = intensity.shape[0]
    size = lax.axis_size("src")
    scale = float(count * size) ** (-0.25)
    bits = size.bit_length() - 1
    half, quarter, pair_count = wide // 2, wide // 4, pairs.shape[1]
    vmem = pl.BlockSpec(memory_space=pltpu.VMEM)
    dma = pltpu.SemaphoreType.DMA
    return pl.pallas_call(
        lambda *refs: kernel(size, scale, *refs),
        out_shape=jax.ShapeDtypeStruct((TIME_STEPS, 2, pair_count), F32),
        in_specs=[pl.BlockSpec(memory_space=pltpu.SMEM)] + [vmem] * 7,
        out_specs=vmem,
        scratch_shapes=[
            pltpu.VMEM((size, beam.shape[1], wide), BF),
            pltpu.VMEM((4, 2, pair_count), jnp.int32),
            pltpu.VMEM((wide, 48), BF),
            pltpu.VMEM((8, wide), F32),
            pltpu.VMEM((wide, 128), F32),
            pltpu.VMEM((2, 48, CHUNK), F32),
            pltpu.VMEM((wide, SLOTS), BF),
            pltpu.VMEM((1, count), F32),
            pltpu.VMEM((2 * wide, CHUNK), BF),
            pltpu.VMEM((2 * wide, CHUNK), BF),
            pltpu.VMEM((2 * wide, 2 * wide), F32),
            pltpu.VMEM((TIME_STEPS, rows, count), F32),
            pltpu.VMEM((TIME_STEPS, rows, count), F32),
            pltpu.VMEM((TIME_STEPS, wide, wide), F32),
            pltpu.VMEM((4, 2, wide, pair_count), BF),
            pltpu.VMEM((TIME_STEPS, half, wide), F32),
            pltpu.VMEM((TIME_STEPS, quarter, wide), BF),
            pltpu.VMEM((TIME_STEPS, quarter, wide), BF),
            pltpu.VMEM((TIME_STEPS, quarter, wide), F32),
            pltpu.VMEM((bits - 2, TIME_STEPS, quarter, wide), BF),
            pltpu.VMEM((bits - 2, TIME_STEPS, quarter, wide), BF),
            pltpu.VMEM((4, 2 * TIME_STEPS, pair_count), F32),
            pltpu.VMEM((3, 2 * TIME_STEPS, pair_count), F32),
            dma((2, bits)),
            dma((2, 3)),
            dma((2, TIME_STEPS)),
            dma((2, TIME_STEPS)),
            dma((2, bits - 2, TIME_STEPS)),
            dma((2, 3)),
        ],
        compiler_params=pltpu.CompilerParams(
            collective_id=0, has_side_effects=True, vmem_limit_bytes=56 * 1024 * 1024
        ),
    )(need, intensity.reshape(1, count), directions, positions, beam, knot_index, knot_weight, pairs)


def solution(mesh):
    placed = (
        P(("chan", "src")),
        P(None, None, "src"),
        P("chan", None),
        P(None, "src"),
        P(None, "src"),
        P(None, None, "src"),
        P(None, None, "src"),
        P(None, "src"),
    )
    return jax.shard_map(
        local, mesh=mesh, in_specs=placed, out_specs=P("chan", None, "src"), check_vma=False
    )
```

```python
import jax
import jax.numpy as jnp
from jax import lax
from jax.experimental import pallas as pl
from jax.experimental.pallas import tpu as pltpu
from jax.sharding import PartitionSpec as P

TIME_STEPS = 4
PATCH_PIXELS = 16
NEED = 8
KNOTS = 4
SLOTS = NEED * PATCH_PIXELS
CHUNK = 512
BF = jnp.bfloat16
F32 = jnp.float32
MAGIC = 12582912.0

SIN = (4.4428679, -7.30744342, 3.59478805, -0.78437398)
COS = (-1.41420408, 6.97764205, -5.71523832, 1.72834847)


def nt(a, b):
    return lax.dot_general(a, b, (((1,), (1,)), ((), ())), preferred_element_type=F32)


def pieces(x):
    hi = x.astype(BF).astype(F32)
    mid = (x - hi).astype(BF).astype(F32)
    return hi, mid, (x - hi) - mid


def partners(size):
    me = lax.axis_index("src")
    flips = [1 << bit for bit in range(size.bit_length() - 1)]
    return me, flips


def flip(me, value):
    return me + value - 2 * value * (lax.div(me, value) % 2)


def greet(others):
    barrier = pltpu.get_barrier_semaphore()
    for other in others:
        pl.semaphore_signal(barrier, inc=1, device_id={"src": other}, device_id_type=pl.DeviceIdType.MESH)
    pl.semaphore_wait(barrier, len(others))


def push(src, dst, send, recv, other):
    copy = pltpu.make_async_remote_copy(
        src_ref=src, dst_ref=dst, send_sem=send, recv_sem=recv,
        device_id={"src": other}, device_id_type=pl.DeviceIdType.MESH,
    )
    copy.start()
    return copy


def reverse(index, bits):
    out = 0
    for bit in range(bits):
        out = out + (index // (1 << bit)) % 2 * (1 << (bits - 1 - bit))
    return out


def kernel(size, scale, need_ref, intensity_ref, directions_ref, positions_ref, beam_ref, index_ref, weight_ref,
           pairs_ref, out_ref, whole, quads, pos, padded, block, dirs, beam_sel, amp, s0, s1, gram, kept_s, kept_n, part,
           ones, got0, send1, got1, acc, sends, gots, res, got, gsem, qsem, sem0, sem1, sems, rsem):
    me, flips = partners(size)
    bits = len(flips)
    count = intensity_ref.shape[1]
    chunks = count // CHUNK
    ants = positions_ref.shape[1]
    depth = beam_ref.shape[1]
    parts = depth // PATCH_PIXELS
    rows, wide = -(-ants // 16) * 16, whole.shape[2]
    half, quarter = wide // 2, wide // 4
    pair_count = pairs_ref.shape[1]
    core, side = me % 2, me // 2 % 2
    quad = [flip(me, 1), flip(me, 2), flip(flip(me, 1), 2)]

    slot_me = reverse(me, bits)
    block[...] = jnp.zeros_like(block)
    block[:ants, :depth] = beam_ref[...].astype(F32)
    whole[slot_me] = block[...].T[:depth].astype(BF)
    quads[me % 4] = pairs_ref[...]
    greet([flip(me, value) for value in flips[2:]] + quad)

    def gather_copy(stage):
        held = 1 << stage
        blocks = whole.at[pl.ds(slot_me // held * held, held)]
        return pltpu.make_async_remote_copy(
            src_ref=blocks, dst_ref=blocks, send_sem=gsem.at[0, stage], recv_sem=gsem.at[1, stage],
            device_id={"src": flip(me, flips[bits - 1 - stage])}, device_id_type=pl.DeviceIdType.MESH,
        )

    gather_copy(0).start()
    listed = [
        push(pairs_ref, quads.at[me % 4], qsem.at[0, j], qsem.at[1, j], other) for j, other in enumerate(quad)
    ]

    amp[...] = jnp.sqrt(intensity_ref[...]) * scale
    s0[...] = jnp.zeros_like(s0)
    s1[...] = jnp.zeros_like(s1)
    gram[...] = jnp.zeros_like(gram)
    dirs[...] = jnp.zeros_like(dirs)
    padded[...] = jnp.zeros_like(padded)
    padded[0:3, :ants] = positions_ref[...]
    p0, p1, p2 = pieces(padded[...])
    pos[...] = jnp.concatenate([p0, p0, p1, p1, p0, p2], axis=0).T.astype(BF)
    slots = (s0, s1)
    iota = lax.broadcasted_iota(jnp.int32, (SLOTS, CHUNK), 0)

    def fringe(t, c, which):
        lanes = pl.ds(pl.multiple_of(c * CHUNK, CHUNK), CHUNK)
        d0, d1, d2 = pieces(directions_ref[t, :, lanes])
        for j, d in enumerate((d0, d1, d0, d1, d2, d0)):
            dirs[which, 8 * j : 8 * j + 3] = d
        u = jnp.dot(pos[:rows], dirs[which].astype(BF), preferred_element_type=F32)
        r = u - ((u + MAGIC) - MAGIC)
        z = r * r
        s = (((SIN[3] * z + SIN[2]) * z + SIN[1]) * z + SIN[0]) * r
        n = ((COS[3] * z + COS[2]) * z + COS[1]) * z + COS[0]
        kept_s[t, :, lanes] = s
        kept_n[t, :, lanes] = n

    def fill(t, c, slot):
        lanes = pl.ds(c * CHUNK, CHUNK)
        spread = jnp.zeros((SLOTS, CHUNK), F32)
        a = amp[:, lanes]
        for k in range(KNOTS):
            w = weight_ref[t, pl.ds(k, 1), lanes] * a
            spread = spread + jnp.where(iota == index_ref[t, pl.ds(k, 1), lanes], w, 0.0)
        hi = spread.astype(BF)
        lo = (spread - hi.astype(F32)).astype(BF)
        b = beam_sel[:rows]
        amount = jnp.dot(
            jnp.concatenate([b, b], axis=1), jnp.concatenate([hi, lo], axis=0), preferred_element_type=F32
        )
        s, n = kept_s[t, :, lanes], kept_n[t, :, lanes]
        q = amount * s
        slot[:rows] = (amount - q * s).astype(BF)
        slot[wide : wide + rows] = (q * n).astype(BF)

    def add(slot):
        for lo in range(0, 2 * wide, 256):
            hi = min(lo + 256, 2 * wide)
            cols = slot[lo:hi]
            if lo < rows:
                gram[lo:rows, lo:hi] += nt(slot[lo:rows], cols)
            top = max(lo, wide)
            gram[top : wide + rows, lo:hi] += nt(slot[top : wide + rows], cols)

    def finish(t):
        w = gram[wide:, :wide]
        real = gram[:wide, :wide] + gram[wide:, wide:]
        r = lax.broadcasted_iota(jnp.int32, (wide, wide), 0)
        c = lax.broadcasted_iota(jnp.int32, (wide, wide), 1)
        part[t] = jnp.where(r > c, real, w - w.T)
        gram[...] = jnp.zeros_like(gram)

    mine = pl.multiple_of(core * half + side * quarter, 32)
    theirs = pl.multiple_of(core * half + (1 - side) * quarter, 32)
    in_mine = pl.multiple_of(side * quarter, 32)
    in_theirs = pl.multiple_of((1 - side) * quarter, 32)

    def remote(src, dst, send, recv, other):
        return pltpu.make_async_remote_copy(
            src_ref=src, dst_ref=dst, send_sem=send, recv_sem=recv,
            device_id={"src": other}, device_id_type=pl.DeviceIdType.MESH,
        )

    def core_copy(t):
        away = part.at[t, pl.ds(pl.multiple_of((1 - core) * half, 64), half)]
        return remote(away, got0.at[t], sem0.at[0, t], sem0.at[1, t], quad[0])

    def side_copy(t):
        return remote(send1.at[t], got1.at[t], sem1.at[0, t], sem1.at[1, t], quad[1])

    def far_copy(t, e):
        return remote(
            sends.at[e, t], gots.at[e, t], sems.at[0, e, t], sems.at[1, e, t], flip(me, flips[2 + e])
        )

    def to_side(t):
        core_copy(t).wait()
        send1[t] = (part[t, pl.ds(theirs, quarter)] + got0[t, pl.ds(in_theirs, quarter)]).astype(BF)
        side_copy(t).start()
        acc[t] = part[t, pl.ds(mine, quarter)] + got0[t, pl.ds(in_mine, quarter)]

    def to_far(t, e):
        if e == 0:
            side_copy(t).wait()
            v = acc[t] + got1[t].astype(F32)
        else:
            far_copy(t, e - 1).wait()
            v = acc[t] + gots[e - 1, t].astype(F32)
        acc[t] = v
        sends[e, t] = v.astype(BF)
        far_copy(t, e).start()

    for stage in range(max(bits, TIME_STEPS)):
        if stage < TIME_STEPS:

            def some(c, carry, t=stage):
                fringe(t, 2 * c, 0)
                fringe(t, 2 * c + 1, 1)
                return carry

            lax.fori_loop(0, chunks // 2, some, 0)
        if stage < bits:
            gather_copy(stage).wait()
            if stage + 1 < bits:
                gather_copy(stage + 1).start()
    for copy in listed:
        copy.wait()

    pair_iota = lax.broadcasted_iota(jnp.int32, (wide, pair_count), 0)

    pixel = lax.broadcasted_iota(jnp.int32, (PATCH_PIXELS, size * depth), 1)
    row = lax.broadcasted_iota(jnp.int32, (PATCH_PIXELS, size * depth), 0)

    def choose(t):
        picked = []
        for j in range(NEED):
            patch = need_ref[t, j]
            at = reverse(patch // parts, bits) * depth + patch % parts * PATCH_PIXELS
            picked.append(jnp.where(pixel - row == at, 1.0, 0.0))
        hot = jnp.concatenate(picked, axis=0).astype(BF)
        got_rows = jnp.dot(hot, whole[...].reshape(size * depth, wide), preferred_element_type=F32)
        beam_sel[...] = got_rows.T.astype(BF)
        for k in range(2):
            ones[t, k] = jnp.where(pair_iota == quads[t, k : k + 1, :], 1.0, 0.0).astype(BF)

    choose(0)
    for c in range(chunks):
        fill(0, c, slots[c % 2])
        if c > 0:
            add(slots[(c + 1) % 2])

    def body(t, carry):
        choose(t)
        for c in range(chunks):
            fill(t, c, slots[c % 2])
            add(slots[(c + 1) % 2])
            if c == 0:
                finish(t - 1)
                core_copy(t - 1).start()

                @pl.when(t > 1)
                def _():
                    to_far(t - 2, 0)
            if c == 2:
                to_side(t - 1)

                @pl.when(t > 1)
                def _():
                    to_far(t - 2, 1)
        return carry

    lax.fori_loop(1, TIME_STEPS, body, 0)
    add(slots[(chunks - 1) % 2])
    finish(TIME_STEPS - 1)
    core_copy(TIME_STEPS - 1).start()
    far = bits - 2
    to_far(TIME_STEPS - 2, 0)
    to_side(TIME_STEPS - 1)
    to_far(TIME_STEPS - 2, 1)
    to_far(TIME_STEPS - 1, 0)
    to_far(TIME_STEPS - 1, 1)
    for e in range(2, far):
        for t in range(TIME_STEPS):
            to_far(t, e)
    local_iota = lax.broadcasted_iota(jnp.int32, (quarter, pair_count), 0) + mine

    def look_up(low, high):
        for t in range(low, high):
            far_copy(t, far - 1).wait()
        total = acc[low:high] + gots[far - 1, low:high].astype(F32)
        total = total.astype(BF).reshape((high - low) * quarter, wide)
        for m in range(4):
            for k in range(2):
                x = jnp.dot(total, ones[m, 1 - k], preferred_element_type=F32)
                mask = local_iota == quads[m, k : k + 1, :]
                for t in range(low, high):
                    y = jnp.where(mask, x[(t - low) * quarter : (t - low + 1) * quarter], 0.0)
                    res[m, 2 * t + 1 - k : 2 * t + 2 - k, :] = jnp.sum(y, axis=0, keepdims=True)

    look_up(0, TIME_STEPS - 1)
    look_up(TIME_STEPS - 1, TIME_STEPS)
    last = []
    for j, other in enumerate(quad):
        last.append(push(res.at[other % 4], got.at[j], rsem.at[0, j], rsem.at[1, j], other))
    for copy in last:
        copy.wait()
    values = res[me % 4] + got[0] + got[1] + got[2]
    for i in range(2 * TIME_STEPS):
        out_ref[i // 2, i % 2 : i % 2 + 1, :] = values[i : i + 1]


def local(intensity, directions, positions, beam, need, knot_index, knot_weight, pairs):
    ants = positions.shape[1]
    rows = -(-ants // 16) * 16
    wide = -(-ants // 128) * 128
    count = intensity.shape[0]
    size = lax.axis_size("src")
    scale = float(count * size) ** (-0.25)
    bits = size.bit_length() - 1
    half, quarter, pair_count = wide // 2, wide // 4, pairs.shape[1]
    vmem = pl.BlockSpec(memory_space=pltpu.VMEM)
    dma = pltpu.SemaphoreType.DMA
    return pl.pallas_call(
        lambda *refs: kernel(size, scale, *refs),
        out_shape=jax.ShapeDtypeStruct((TIME_STEPS, 2, pair_count), F32),
        in_specs=[pl.BlockSpec(memory_space=pltpu.SMEM)] + [vmem] * 7,
        out_specs=vmem,
        scratch_shapes=[
            pltpu.VMEM((size, beam.shape[1], wide), BF),
            pltpu.VMEM((4, 2, pair_count), jnp.int32),
            pltpu.VMEM((wide, 48), BF),
            pltpu.VMEM((8, wide), F32),
            pltpu.VMEM((wide, 128), F32),
            pltpu.VMEM((2, 48, CHUNK), F32),
            pltpu.VMEM((wide, SLOTS), BF),
            pltpu.VMEM((1, count), F32),
            pltpu.VMEM((2 * wide, CHUNK), BF),
            pltpu.VMEM((2 * wide, CHUNK), BF),
            pltpu.VMEM((2 * wide, 2 * wide), F32),
            pltpu.VMEM((TIME_STEPS, rows, count), F32),
            pltpu.VMEM((TIME_STEPS, rows, count), F32),
            pltpu.VMEM((TIME_STEPS, wide, wide), F32),
            pltpu.VMEM((4, 2, wide, pair_count), BF),
            pltpu.VMEM((TIME_STEPS, half, wide), F32),
            pltpu.VMEM((TIME_STEPS, quarter, wide), BF),
            pltpu.VMEM((TIME_STEPS, quarter, wide), BF),
            pltpu.VMEM((TIME_STEPS, quarter, wide), F32),
            pltpu.VMEM((bits - 2, TIME_STEPS, quarter, wide), BF),
            pltpu.VMEM((bits - 2, TIME_STEPS, quarter, wide), BF),
            pltpu.VMEM((4, 2 * TIME_STEPS, pair_count), F32),
            pltpu.VMEM((3, 2 * TIME_STEPS, pair_count), F32),
            dma((2, bits)),
            dma((2, 3)),
            dma((2, TIME_STEPS)),
            dma((2, TIME_STEPS)),
            dma((2, bits - 2, TIME_STEPS)),
            dma((2, 3)),
        ],
        compiler_params=pltpu.CompilerParams(
            collective_id=0, has_side_effects=True, vmem_limit_bytes=56 * 1024 * 1024
        ),
    )(need, intensity.reshape(1, count), directions, positions, beam, knot_index, knot_weight, pairs)


def solution(mesh):
    placed = (
        P(("chan", "src")),
        P(None, None, "src"),
        P("chan", None),
        P(None, "src"),
        P(None, "src"),
        P(None, None, "src"),
        P(None, None, "src"),
        P(None, "src"),
    )
    return jax.shard_map(
        local, mesh=mesh, in_specs=placed, out_specs=P("chan", None, "src"), check_vma=False
    )
```
